128 devices in a mesh: base: 8 (over z, x_lo), inst: 16 (over y, x_hi, core).
Axes of the slice: x: 4 (x_hi: 2, x_lo: 2; x = x_hi * 2 + x_lo), y: 4, z: 4, core: 2. Of those that a mesh axis runs over, the one named last changes fastest.
Arguments:
- base_pre: bfloat16 [4096, 16384], P(('base', 'inst'))
- inst_pre: bfloat16 [4096, 16384], P(('base', 'inst'))
- base_support: int32 [4096, 128], P(('base', 'inst')), may hold values from 0 to 16383, all different within a row
- inst_support: int32 [4096, 128], P(('base', 'inst')), may hold values from 0 to 16383, all different within a row
Outputs:
- scores: float32 [16384, 16384], P('base', 'inst')
The draws below stay inside these ranges and needn't reach their ends.
Inputs may be any that keep to these rules, and one draw needn't show every extreme that they name: `base_support`: the 128 indices of a row are distinct latents. `inst_support`: the 128 indices of a row are distinct latents.
All inputs are finite; a program needn't handle non-finite values.
Results may differ from the reference program's by a relative error of at most 0.004.
Values may be sent and summed in bfloat16 or wider, within the bound.
No kernel may reach another device: no remote copies, remote signals or barrier semaphores. Data moves between devices by JAX's collectives and lax.ppermute only.
A program may use at most 128 MiB of HBM per device.

```python
import jax
import jax.numpy as jnp
from jax import lax

L = 16384
K = 128
TOKENS = 4096


def latent_values(key, top_scale):
    scale_key, value_key = jax.random.split(key)
    scales = jnp.exp(jax.random.uniform(scale_key, (L,), jnp.float32, 0.0, jnp.log(top_scale)))
    values = jax.random.normal(value_key, (TOKENS, L), jnp.float32)
    return values * scales[None, :]


def draw_base_pre(key, part):
    key = jax.random.fold_in(key, 11)
    return latent_values(key, 10.0).astype(jnp.bfloat16)


def draw_inst_pre(key, part):
    key = jax.random.fold_in(key, 23)
    return latent_values(key, 10.0).astype(jnp.bfloat16)


def picks_of(own_key, rows, number_of, top, lift):
    ranking = jax.random.permutation(jax.random.fold_in(own_key, 1), number_of)
    favour = ranking
    for power in range(3):
        favour = favour * favour // number_of
    favour = favour * lift // number_of
    chance = jax.random.randint(jax.random.fold_in(own_key, 2), (rows, number_of), 0, 4096) + favour
    sure = jax.random.permutation(jax.random.fold_in(own_key, 3), rows)[jnp.arange(number_of) % rows]
    chance = jnp.where(jnp.arange(rows)[:, None] == sure[None, :], 1 << 14, chance)
    merit = chance * number_of + jnp.arange(number_of)
    return lax.top_k(merit.astype(jnp.int32), top)[1].astype(jnp.int32)


def setup_inputs(seed: int = 0) -> dict:
    seeds = jax.random.split(jax.random.key(seed), 5)
    return {
        "base_pre": draw_base_pre(jax.random.fold_in(seeds[4], 71), 0),
        "inst_pre": draw_inst_pre(jax.random.fold_in(seeds[4], 71), 0),
        "base_support": picks_of(seeds[2], TOKENS, L, K, 64),
        "inst_support": picks_of(seeds[3], TOKENS, L, K, 64),
    }


def emphasize(pre, support):
    pre32 = pre.astype(jnp.float32)
    scale = lax.rsqrt(lax.optimization_barrier(jnp.mean(pre32 * pre32, axis=1, keepdims=True)) + 1e-06)
    rows = jnp.arange(pre.shape[0], dtype=jnp.int32)[:, None]
    active = jnp.zeros(pre.shape, jnp.float32).at[rows, support].set(1.0)
    return (pre32 * scale * (1.0 + 3.0 * active)).astype(jnp.bfloat16)

def reference(base_pre, inst_pre, base_support, inst_support):
    base_codes = emphasize(base_pre, base_support)
    inst_codes = emphasize(inst_pre, inst_support)
    gram = lax.dot_general(base_codes, inst_codes, (((0,), (0,)), ((), ())), preferred_element_type=jnp.float32)
    base32 = base_codes.astype(jnp.float32)
    inst32 = inst_codes.astype(jnp.float32)
    total = base_codes.shape[0]
    base_rms = jnp.sqrt(lax.optimization_barrier(jnp.sum(base32 * base32, axis=0)) / total + 1e-06)
    inst_rms = jnp.sqrt(lax.optimization_barrier(jnp.sum(inst32 * inst32, axis=0)) / total + 1e-06)
    return gram / (jnp.sqrt(jnp.float32(total)) * base_rms[:, None] * inst_rms[None, :])
```

```python
import functools

import jax
import jax.numpy as jnp
from jax import lax
from jax.experimental import pallas as pl
from jax.experimental.pallas import tpu as pltpu
from jax.sharding import Mesh
from jax.sharding import PartitionSpec as P

AXES = ("z", "xl", "y", "xh", "c")
SIZES = (4, 2, 4, 2, 2)
TILE = 256


def emphasize_kernel(pre_ref, support_ref, out_ref, mask_ref):
    toks, latents = pre_ref.shape
    active = support_ref.shape[1]
    groups = latents // 128
    per_block = out_ref.shape[2] // 128
    rows = lax.broadcasted_iota(jnp.int32, (groups, active), 0)
    lanes = lax.broadcasted_iota(jnp.int32, (128, active), 0)

    def token(t, carry):
        picks = support_ref[pl.ds(t, 1), :]
        high = (rows == (picks >> 7)).astype(jnp.bfloat16)
        low = (lanes == (picks & 127)).astype(jnp.bfloat16)
        mask_ref[pl.ds(t * groups, groups), :] = lax.dot_general(
            high, low, (((1,), (1,)), ((), ())), preferred_element_type=jnp.float32
        )
        return carry

    lax.fori_loop(0, toks, token, 0, unroll=4)
    total = jnp.zeros((toks, 128), jnp.float32)
    for g in range(groups):
        wide = pre_ref[:, g * 128 : (g + 1) * 128].astype(jnp.float32)
        total = total + wide * wide
    scale = lax.rsqrt(jnp.sum(total, axis=1, keepdims=True) / latents + 1e-06)
    for g in range(groups):
        wide = pre_ref[:, g * 128 : (g + 1) * 128].astype(jnp.float32)
        on = mask_ref[pl.ds(g, toks, stride=groups), :]
        block, place = g // per_block, g % per_block * 128
        out_ref[block, :, place : place + 128] = (wide * scale * (1.0 + 3.0 * on)).astype(jnp.bfloat16)


def emphasize(pre, support, blocks):
    toks, latents = pre.shape
    return pl.pallas_call(
        emphasize_kernel,
        out_shape=jax.ShapeDtypeStruct((blocks, toks, latents // blocks), jnp.bfloat16),
        in_specs=[pl.BlockSpec(memory_space=pltpu.VMEM)] * 2,
        out_specs=pl.BlockSpec(memory_space=pltpu.VMEM),
        scratch_shapes=[pltpu.VMEM((toks * (latents // 128), 128), jnp.float32)],
        compiler_params=pltpu.CompilerParams(vmem_limit_bytes=24 << 20),
        cost_estimate=pl.CostEstimate(flops=1 << 30, bytes_accessed=4 << 20, transcendentals=0),
        name="emphasize",
    )(pre, support)


def dot_kernel(combos, base_keys, inst_keys, first, last, total, *refs):
    pos = refs[0]
    base = dict(zip(base_keys, refs[1 : 1 + len(base_keys)]))
    refs = refs[1 + len(base_keys) :]
    inst = dict(zip(inst_keys, refs[: len(inst_keys)]))
    refs = refs[len(inst_keys) :]
    if not first:
        acc_ref, bsq_ref, isq_ref, *refs = refs
    if last:
        out_ref, rhs_ref, isum_ref = refs
    else:
        out_ref, bsq_out, isq_out, rhs_ref, isum_ref = refs
    z, xl, y, xh, c = (pos[i] for i in range(5))
    order = [
        (dy, dz, dxl, dxh, dc)
        for dy, dz in combos
        for dxl in range(2)
        for dxh in range(2)
        for dc in range(2)
    ]

    @pl.when(pl.program_id(0) == 0)
    def _():
        sums = jnp.zeros((8, rhs_ref.shape[1]), jnp.float32)
        for n, (dy, dz, dxl, dxh, dc) in enumerate(order):
            place = ((y + dy) & 3) * 4 + (xh ^ dxh) * 2 + (c ^ dc)
            rows = inst[dz, dxl][place]
            rhs_ref[n * 32 : (n + 1) * 32, :] = rows
            wide = rows.astype(jnp.float32)
            sums = sums + jnp.sum((wide * wide).reshape(4, 8, -1), axis=0)
        sums = jnp.sum(sums, axis=0, keepdims=True)
        if not first:
            sums = sums + isq_ref[...]
        isum_ref[...] = sums

    blocks = []
    sums = jnp.zeros((8, TILE), jnp.float32)
    whole = base[base_keys[0]].shape[0] == 4
    for dy, dz, dxl, dxh, dc in order:
        rows = base[dy, dxh, dc][((z + dz) & 3) if whole else 0, xl ^ dxl]
        blocks.append(rows)
        wide = rows.astype(jnp.float32)
        sums = sums + jnp.sum((wide * wide).reshape(4, 8, -1), axis=0)
    sums = jnp.sum(sums, axis=0, keepdims=True)
    if not first:
        sums = sums + bsq_ref[...]
    gram = lax.dot_general(
        jnp.concatenate(blocks, axis=0),
        rhs_ref[...],
        (((0,), (0,)), ((), ())),
        preferred_element_type=jnp.float32,
    )
    if not first:
        gram = gram + acc_ref[...]
    if last:
        base_inv = 1.0 / (jnp.sqrt(sums / total + 1e-06) * jnp.sqrt(jnp.float32(total)))
        inst_inv = 1.0 / jnp.sqrt(isum_ref[...] / total + 1e-06)
        column = jnp.transpose(jnp.broadcast_to(base_inv, (8, TILE)))[:, :1]
        out_ref[...] = gram * column * inst_inv
    else:
        out_ref[...] = gram
        bsq_out[...] = sums
        isq_out[...] = isum_ref[...]


def partial_gram(pos, base, inst, combos, carry, last, total):
    base_keys = [k for k in base if k[0] in {dy for dy, _ in combos}]
    dzs = sorted({dz for _, dz in combos})
    inst_keys = [k for k in inst if k[0] in dzs]
    first = carry is None
    m = base[base_keys[0]].shape[-1]
    n = inst[inst_keys[0]].shape[-1]
    if len(dzs) == 1:
        base_spec = pl.BlockSpec((1, 2, 32, TILE), lambda i, p: ((p[0] + dzs[0]) & 3, 0, 0, i))
    else:
        base_spec = pl.BlockSpec((4, 2, 32, TILE), lambda i, p: (0, 0, 0, i))
    inst_spec = pl.BlockSpec((16, 32, n), lambda i, p: (0, 0, 0))
    gram_spec = pl.BlockSpec((TILE, n), lambda i, p: (i, 0))
    bsq_spec = pl.BlockSpec((1, TILE), lambda i, p: (0, i))
    isq_spec = pl.BlockSpec((1, n), lambda i, p: (0, 0))
    carry_specs = [gram_spec, bsq_spec, isq_spec]
    carry_shapes = [
        jax.ShapeDtypeStruct((m, n), jnp.float32),
        jax.ShapeDtypeStruct((1, m), jnp.float32),
        jax.ShapeDtypeStruct((1, n), jnp.float32),
    ]
    depth = len(combos) * 256
    return pl.pallas_call(
        functools.partial(dot_kernel, combos, base_keys, inst_keys, first, last, total),
        grid_spec=pltpu.PrefetchScalarGridSpec(
            num_scalar_prefetch=1,
            grid=(m // TILE,),
            in_specs=[base_spec] * len(base_keys)
            + [inst_spec] * len(inst_keys)
            + ([] if first else carry_specs),
            out_specs=gram_spec if last else carry_specs,
            scratch_shapes=[pltpu.VMEM((depth, n), jnp.bfloat16), pltpu.VMEM((1, n), jnp.float32)],
        ),
        out_shape=carry_shapes[0] if last else carry_shapes,
        compiler_params=pltpu.CompilerParams(vmem_limit_bytes=56 << 20),
        cost_estimate=pl.CostEstimate(
            flops=2 * depth * m * n, bytes_accessed=depth * (m + n) * 2 + 8 * m * n, transcendentals=0
        ),
        name="partial_gram",
    )(
        pos,
        *[base[k].reshape(4, 2, 32, m) for k in base_keys],
        *[inst[k] for k in inst_keys],
        *([] if first else carry),
    )


def shift(x, axis, step):
    size = lax.axis_size(axis)
    return lax.ppermute(x, axis, [(i, (i + step) % size) for i in range(size)])


def ring_gather(own, pair_axis, ring_axis):
    other = shift(own, pair_axis, 1)
    got = {(0, 0): own, (0, 1): other}
    for key, x in ((0, own), (1, other)):
        got[3, key] = shift(x, ring_axis, 1)
        got[1, key] = shift(x, ring_axis, -1)
    got[2, 0] = shift(got[3, 0], ring_axis, 1)
    got[2, 1] = shift(got[1, 1], ring_axis, -1)
    return got


def per_device(base_pre, inst_pre, base_support, inst_support):
    total = base_pre.shape[0] * 128
    pos = jnp.stack([lax.axis_index(a) for a in AXES]).astype(jnp.int32)
    base_codes = emphasize(base_pre, base_support, 8)
    base_own = lax.all_to_all(base_codes, ("z", "xl"), 0, 0, tiled=True)
    inst_codes = emphasize(inst_pre, inst_support, 16)
    inst_own = lax.all_to_all(inst_codes, ("y", "xh", "c"), 0, 0, tiled=True)
    base_got = ring_gather(base_own, "xh", "y")
    inst = ring_gather(inst_own, "xl", "z")
    base = {}
    for (dy, dxh), x in base_got.items():
        base[dy, dxh, 0] = x
        base[dy, dxh, 1] = shift(x, "c", 1)
    near = (0, 1, 3)
    carry = partial_gram(pos, base, inst, [(dy, dz) for dy in near for dz in near], None, False, total)
    carry = partial_gram(pos, base, inst, [(2, dz) for dz in near], carry, False, total)
    return partial_gram(pos, base, inst, [(dy, 2) for dy in range(4)], carry, True, total)


def solution(mesh):
    split = Mesh(mesh.devices.reshape(SIZES), AXES)
    spec = P(AXES, None)
    return jax.shard_map(
        per_device,
        mesh=split,
        in_specs=(spec,) * 4,
        out_specs=P(("z", "xl"), ("y", "xh", "c")),
        check_vma=False,
    )
```

```python
import functools

import jax
import jax.numpy as jnp
from jax import lax
from jax.experimental import pallas as pl
from jax.experimental.pallas import tpu as pltpu
from jax.sharding import PartitionSpec as P

AXES = ("base", "inst")
SIZES = (4, 2, 4, 2, 2)
TILE = 512
ROWS = 32


def device(z, xl, y, xh, c):
    return (((z % 4) * 2 + xl) * 4 + y % 4) * 4 + xh * 2 + c


def places():
    return [(z, xl, y, xh, c) for z in range(4) for xl in range(2) for y in range(4) for xh in range(2) for c in range(2)]


def emphasize_kernel(side, pos_ref, base_ref, inst_ref, base_sup_ref, inst_sup_ref, out_ref, pre_ref, support_ref, mask_ref, sem):
    for own, pre, sup in ((side, base_ref, base_sup_ref), (1 - side, inst_ref, inst_sup_ref)):

        @pl.when(pos_ref[4] == own)
        def _(pre=pre, sup=sup):
            pltpu.make_async_copy(sup, support_ref, sem.at[0]).start()
            pltpu.make_async_copy(pre, pre_ref, sem.at[1]).start()

    pltpu.make_async_copy(base_sup_ref, support_ref, sem.at[0]).wait()
    toks, latents = pre_ref.shape
    active = support_ref.shape[1]
    groups = latents // 128
    per_block = groups // 8
    rows = lax.broadcasted_iota(jnp.int32, (groups, active), 0)
    lanes = lax.broadcasted_iota(jnp.int32, (128, active), 0)

    def token(t, carry):
        picks = support_ref[pl.ds(t, 1), :]
        high = (rows == (picks >> 7)).astype(jnp.bfloat16)
        low = (lanes == (picks & 127)).astype(jnp.bfloat16)
        mask_ref[pl.ds(t * groups, groups), :] = lax.dot_general(
            high, low, (((1,), (1,)), ((), ())), preferred_element_type=jnp.float32
        )
        return carry

    lax.fori_loop(0, toks, token, 0, unroll=8)
    pltpu.make_async_copy(base_ref, pre_ref, sem.at[1]).wait()
    total = jnp.zeros((toks, 128), jnp.float32)
    for g in range(groups):
        wide = pre_ref[:, g * 128 : (g + 1) * 128].astype(jnp.float32)
        total = total + wide * wide
    scale = lax.rsqrt(jnp.sum(total, axis=1, keepdims=True) / latents + 1e-06)
    for g in range(groups):
        wide = pre_ref[:, g * 128 : (g + 1) * 128].astype(jnp.float32)
        on = mask_ref[pl.ds(g, toks, stride=groups), :]
        block, place = g // per_block, g % per_block * 128
        out_ref[block, :, place : place + 128] = (wide * scale * (1.0 + 3.0 * on)).astype(jnp.bfloat16)


def emphasize(side, pos, base_pre, inst_pre, base_support, inst_support):
    toks, latents = base_pre.shape
    return pl.pallas_call(
        functools.partial(emphasize_kernel, side),
        out_shape=jax.ShapeDtypeStruct((8, toks, latents // 8), jnp.bfloat16),
        in_specs=[pl.BlockSpec(memory_space=pltpu.SMEM)] + [pl.BlockSpec(memory_space=pl.ANY)] * 4,
        out_specs=pl.BlockSpec(memory_space=pltpu.VMEM),
        scratch_shapes=[
            pltpu.VMEM(base_pre.shape, base_pre.dtype),
            pltpu.VMEM(base_support.shape, base_support.dtype),
            pltpu.VMEM((toks * (latents // 128), 128), jnp.float32),
            pltpu.SemaphoreType.DMA((2,)),
        ],
        compiler_params=pltpu.CompilerParams(vmem_limit_bytes=56 << 20),
        cost_estimate=pl.CostEstimate(flops=1 << 30, bytes_accessed=4 << 20, transcendentals=0),
        name="emphasize",
    )(pos, base_pre, inst_pre, base_support, inst_support)


def dot_kernel(pairs, base_keys, inst_keys, first, last, total, *refs):
    pos, refs = refs[0], list(refs[1:])
    base = {key: refs.pop(0) for key in base_keys}
    inst = {key: refs.pop(0) for key in inst_keys}
    if not first:
        acc_ref, bsq_ref, isq_ref = refs[:3]
        del refs[:3]
    if last:
        out_ref, rhs_ref, isum_ref, sem = refs
    else:
        out_ref, bsq_out, isq_out, rhs_ref, isum_ref, sem = refs
    z, xl, y, xh, c = (pos[i] for i in range(5))
    n = rhs_ref.shape[1]

    @pl.when(pl.program_id(0) == 0)
    def _():
        columns = pl.ds(pl.multiple_of(c * n, n), n)
        copies = []
        for row, ((dy, dxh, _), key) in enumerate(pairs):
            source = inst[key].at[((y + dy) & 3) * 2 + (xh ^ dxh), :, columns]
            copies.append(pltpu.make_async_copy(source, rhs_ref.at[pl.ds(row * ROWS, ROWS)], sem))
        for copy in copies:
            copy.start()
        for copy in copies:
            copy.wait()
        sums = jnp.zeros((8, n), jnp.float32)
        for row in range(len(pairs)):
            wide = rhs_ref[row * ROWS : (row + 1) * ROWS, :].astype(jnp.float32)
            sums = sums + jnp.sum((wide * wide).reshape(4, 8, -1), axis=0)
        sums = jnp.sum(sums, axis=0, keepdims=True)
        isum_ref[...] = sums if first else sums + isq_ref[...]

    blocks = []
    sums = jnp.zeros((8, TILE), jnp.float32)
    for key, (dz, dxl, _) in pairs:
        rows = base[key][((z + dz) & 3) * 2 + (xl ^ dxl)]
        blocks.append(rows)
        wide = rows.astype(jnp.float32)
        sums = sums + jnp.sum((wide * wide).reshape(4, 8, -1), axis=0)
    sums = jnp.sum(sums, axis=0, keepdims=True)
    if not first:
        sums = sums + bsq_ref[...]
    gram = lax.dot_general(
        jnp.concatenate(blocks, axis=0),
        rhs_ref[...],
        (((0,), (0,)), ((), ())),
        preferred_element_type=jnp.float32,
    )
    if not first:
        gram = gram + acc_ref[...]
    if last:
        base_inv = 1.0 / (jnp.sqrt(sums / total + 1e-06) * jnp.sqrt(jnp.float32(total)))
        inst_inv = 1.0 / jnp.sqrt(isum_ref[...] / total + 1e-06)
        column = jnp.transpose(jnp.broadcast_to(base_inv, (8, TILE)))[:, :1]
        out_ref[...] = gram * column * inst_inv
    else:
        out_ref[...] = gram
        bsq_out[...] = sums
        isq_out[...] = isum_ref[...]


def partial_gram(pos, own, mate, pairs, carry, last, total):
    first = carry is None
    base_keys = sorted({key for key, _ in pairs})
    inst_keys = sorted({key for _, key in pairs})
    m = own[base_keys[0]].shape[-1]
    n = m // 2
    carry_specs = [
        pl.BlockSpec((TILE, n), lambda i, p: (i, 0)),
        pl.BlockSpec((1, TILE), lambda i, p: (0, i)),
        pl.BlockSpec((1, n), lambda i, p: (0, 0)),
    ]
    carry_shapes = [
        jax.ShapeDtypeStruct((m, n), jnp.float32),
        jax.ShapeDtypeStruct((1, m), jnp.float32),
        jax.ShapeDtypeStruct((1, n), jnp.float32),
    ]
    depth = len(pairs) * ROWS
    call = pl.pallas_call(
        functools.partial(dot_kernel, pairs, base_keys, inst_keys, first, last, total),
        grid_spec=pltpu.PrefetchScalarGridSpec(
            num_scalar_prefetch=1,
            grid=(m // TILE,),
            in_specs=[pl.BlockSpec((8, ROWS, TILE), lambda i, p: (0, 0, i))] * len(base_keys)
            + [pl.BlockSpec(memory_space=pl.ANY)] * len(inst_keys)
            + ([] if first else carry_specs),
            out_specs=carry_specs[0] if last else carry_specs,
            scratch_shapes=[
                pltpu.VMEM((depth, n), jnp.bfloat16),
                pltpu.VMEM((1, n), jnp.float32),
                pltpu.SemaphoreType.DMA,
            ],
        ),
        out_shape=carry_shapes[0] if last else carry_shapes,
        compiler_params=pltpu.CompilerParams(vmem_limit_bytes=56 << 20),
        cost_estimate=pl.CostEstimate(
            flops=2 * depth * m * n, bytes_accessed=depth * (m + n) * 2 + 8 * m * n, transcendentals=0
        ),
        name="partial_gram",
    )

    def run(pos, base, inst, carry):
        return call(pos, *[base[k] for k in base_keys], *[inst[k] for k in inst_keys], *(carry or ()))

    keys = set(base_keys + inst_keys)
    own, mate = ({key: pieces[key] for key in keys} for pieces in (own, mate))
    return lax.cond(
        pos[4] == 0,
        lambda pos, own, mate, carry: run(pos, own, mate, carry),
        lambda pos, own, mate, carry: run(pos, mate, own, carry),
        pos,
        own,
        mate,
        carry,
    )


def send(x, target):
    return lax.ppermute(x, AXES, [(device(*p), device(*target(*p))) for p in places()])


def ring(x, way):
    return send(x, lambda z, xl, y, xh, c: (z + way * c, xl, y + way * (1 - c), xh, c))


def across(x):
    return send(x, lambda z, xl, y, xh, c: (z, xl ^ c, y, xh ^ (1 - c), c))


def mated(x):
    return send(x, lambda z, xl, y, xh, c: (z, xl, y, xh, 1 - c))


def per_device(base_pre, inst_pre, base_support, inst_support):
    total = base_pre.shape[0] * 128
    tie = lax.optimization_barrier

    def after(x, *others):
        return tie((x, others))[0]

    row, column = lax.axis_index("base"), lax.axis_index("inst")
    pos = jnp.stack([row // 2, row % 2, column // 4, column // 2 % 2, column % 2]).astype(jnp.int32)
    codes = [base_pre, inst_pre, base_support, inst_support]
    groups = [
        [device(z, xl, y, xh, 0) for z in range(4) for xl in range(2)] for y in range(4) for xh in range(2)
    ] + [[device(z, xl, y, xh, 1) for y in range(4) for xh in range(2)] for z in range(4) for xl in range(2)]

    def spread(x):
        return lax.all_to_all(x, AXES, 0, 0, axis_index_groups=groups, tiled=True)

    staying = emphasize(0, pos, *codes)
    leaving = emphasize(1, after(pos, staying), *codes)
    a = spread(staying)
    leaving, a = tie((leaving, a))
    arriving = mated(leaving)
    a3, a1 = ring(a, 1), ring(a, -1)
    xa = across(a)
    b = spread(arriving)
    a2 = ring(a3, 1)
    b3, b1 = ring(b, 1), ring(b, -1)
    b2 = ring(b1, -1)
    xa = after(xa, b3, b1, a2)
    xb = across(after(b, xa))
    xa3, xa1 = ring(xa, 1), ring(xa, -1)
    xb = after(xb, xa3, xa1, b2)
    xb3, xb1 = ring(xb, 1), ring(xb, -1)
    xa2 = ring(xa3, 1)
    own = {(0, 0, 0): a, (1, 0, 0): a1, (2, 0, 0): a2, (3, 0, 0): a3}
    own |= {(0, 0, 1): b, (1, 0, 1): b1, (2, 0, 1): b2, (3, 0, 1): b3}
    mate = {key: mated(x) for key, x in own.items()}
    steps = [(k, dx) for k in range(4) for dx in range(2)]
    blocks = [(p + (t,), q + (1 - t,)) for t in range(2) for q in steps for p in steps]
    early = [(p, q) for p, q in blocks if p[1] == 0 and q[1] == 0]
    late = [(p, q) for p, q in blocks if (p, q) not in early]
    carry = partial_gram(after(pos, xb), own, mate, early, None, False, total)
    xb3, xb1, carry = tie((xb3, xb1, carry))
    xb2 = ring(xb1, -1)
    more = {(0, 1, 0): xa, (1, 1, 0): xa1, (2, 1, 0): xa2, (3, 1, 0): xa3}
    more |= {(0, 1, 1): xb, (1, 1, 1): xb1, (2, 1, 1): xb2, (3, 1, 1): xb3}
    own |= more
    mate |= {key: mated(x) for key, x in more.items()}
    return partial_gram(pos, own, mate, late, carry, True, total)


def solution(mesh):
    spec = P(AXES, None)
    return jax.shard_map(
        per_device, mesh=mesh, in_specs=(spec,) * 4, out_specs=P("base", "inst"), check_vma=False
    )
```

```python
import functools

import jax
import jax.numpy as jnp
from jax import lax
from jax.experimental import pallas as pl
from jax.experimental.pallas import tpu as pltpu
from jax.sharding import PartitionSpec as P

AXES = ("base", "inst")
SIZES = (4, 2, 4, 2, 2)
TILE = 512
ROWS = 32


def device(z, xl, y, xh, c):
    return (((z % 4) * 2 + xl) * 4 + y % 4) * 4 + xh * 2 + c


def places():
    return [(z, xl, y, xh, c) for z in range(4) for xl in range(2) for y in range(4) for xh in range(2) for c in range(2)]


def emphasize_kernel(side, pos_ref, base_ref, inst_ref, base_sup_ref, inst_sup_ref, out_ref, pre_ref, support_ref, mask_ref, sem):
    for own, pre, sup in ((side, base_ref, base_sup_ref), (1 - side, inst_ref, inst_sup_ref)):

        @pl.when(pos_ref[4] == own)
        def _(pre=pre, sup=sup):
            pltpu.make_async_copy(sup, support_ref, sem.at[0]).start()
            pltpu.make_async_copy(pre, pre_ref, sem.at[1]).start()

    pltpu.make_async_copy(base_sup_ref, support_ref, sem.at[0]).wait()
    toks, latents = pre_ref.shape
    active = support_ref.shape[1]
    groups = latents // 128
    per_block = groups // 8
    rows = lax.broadcasted_iota(jnp.int32, (groups, active), 0)
    lanes = lax.broadcasted_iota(jnp.int32, (128, active), 0)

    def token(t, carry):
        picks = support_ref[pl.ds(t, 1), :]
        high = (rows == (picks >> 7)).astype(jnp.bfloat16)
        low = (lanes == (picks & 127)).astype(jnp.bfloat16)
        mask_ref[pl.ds(t * groups, groups), :] = lax.dot_general(
            high, low, (((1,), (1,)), ((), ())), preferred_element_type=jnp.float32
        )
        return carry

    lax.fori_loop(0, toks, token, 0, unroll=8)
    pltpu.make_async_copy(base_ref, pre_ref, sem.at[1]).wait()
    total = jnp.zeros((toks, 128), jnp.float32)
    for g in range(groups):
        wide = pre_ref[:, g * 128 : (g + 1) * 128].astype(jnp.float32)
        total = total + wide * wide
    scale = lax.rsqrt(jnp.sum(total, axis=1, keepdims=True) / latents + 1e-06)
    for g in range(groups):
        wide = pre_ref[:, g * 128 : (g + 1) * 128].astype(jnp.float32)
        on = mask_ref[pl.ds(g, toks, stride=groups), :]
        block, place = g // per_block, g % per_block * 128
        out_ref[block, :, place : place + 128] = (wide * scale * (1.0 + 3.0 * on)).astype(jnp.bfloat16)


def emphasize(side, pos, base_pre, inst_pre, base_support, inst_support):
    toks, latents = base_pre.shape
    return pl.pallas_call(
        functools.partial(emphasize_kernel, side),
        out_shape=jax.ShapeDtypeStruct((8, toks, latents // 8), jnp.bfloat16),
        in_specs=[pl.BlockSpec(memory_space=pltpu.SMEM)] + [pl.BlockSpec(memory_space=pl.ANY)] * 4,
        out_specs=pl.BlockSpec(memory_space=pltpu.VMEM),
        scratch_shapes=[
            pltpu.VMEM(base_pre.shape, base_pre.dtype),
            pltpu.VMEM(base_support.shape, base_support.dtype),
            pltpu.VMEM((toks * (latents // 128), 128), jnp.float32),
            pltpu.SemaphoreType.DMA((2,)),
        ],
        compiler_params=pltpu.CompilerParams(vmem_limit_bytes=56 << 20),
        cost_estimate=pl.CostEstimate(flops=1 << 30, bytes_accessed=4 << 20, transcendentals=0),
        name="emphasize",
    )(pos, base_pre, inst_pre, base_support, inst_support)


def dot_kernel(pairs, base_keys, inst_keys, first, last, total, *refs):
    pos, refs = refs[0], list(refs[1:])
    base = {key: refs.pop(0) for key in base_keys}
    inst = {key: refs.pop(0) for key in inst_keys}
    if not first:
        acc_ref, bsq_ref, isq_ref = refs[:3]
        del refs[:3]
    if last:
        out_ref, rhs_ref, isum_ref, sem = refs
    else:
        out_ref, bsq_out, isq_out, rhs_ref, isum_ref, sem = refs
    z, xl, y, xh, c = (pos[i] for i in range(5))
    n = rhs_ref.shape[1]

    @pl.when(pl.program_id(0) == 0)
    def _():
        columns = pl.ds(pl.multiple_of(c * n, n), n)
        copies = []
        for row, ((dy, dxh, _), key) in enumerate(pairs):
            source = inst[key].at[((y + dy) & 3) * 2 + (xh ^ dxh), :, columns]
            copies.append(pltpu.make_async_copy(source, rhs_ref.at[pl.ds(row * ROWS, ROWS)], sem))
        for copy in copies:
            copy.start()
        for copy in copies:
            copy.wait()
        sums = jnp.zeros((8, n), jnp.float32)
        for row in range(len(pairs)):
            wide = rhs_ref[row * ROWS : (row + 1) * ROWS, :].astype(jnp.float32)
            sums = sums + jnp.sum((wide * wide).reshape(4, 8, -1), axis=0)
        sums = jnp.sum(sums, axis=0, keepdims=True)
        isum_ref[...] = sums if first else sums + isq_ref[...]

    blocks = []
    sums = jnp.zeros((8, TILE), jnp.float32)
    for key, (dz, dxl, _) in pairs:
        rows = base[key][((z + dz) & 3) * 2 + (xl ^ dxl)]
        blocks.append(rows)
        wide = rows.astype(jnp.float32)
        sums = sums + jnp.sum((wide * wide).reshape(4, 8, -1), axis=0)
    sums = jnp.sum(sums, axis=0, keepdims=True)
    if not first:
        sums = sums + bsq_ref[...]
    gram = lax.dot_general(
        jnp.concatenate(blocks, axis=0),
        rhs_ref[...],
        (((0,), (0,)), ((), ())),
        preferred_element_type=jnp.float32,
    )
    if not first:
        gram = gram + acc_ref[...]
    if last:
        base_inv = 1.0 / (jnp.sqrt(sums / total + 1e-06) * jnp.sqrt(jnp.float32(total)))
        inst_inv = 1.0 / jnp.sqrt(isum_ref[...] / total + 1e-06)
        column = jnp.transpose(jnp.broadcast_to(base_inv, (8, TILE)))[:, :1]
        out_ref[...] = gram * column * inst_inv
    else:
        out_ref[...] = gram
        bsq_out[...] = sums
        isq_out[...] = isum_ref[...]


def partial_gram(pos, own, mate, pairs, carry, last, total):
    first = carry is None
    base_keys = sorted({key for key, _ in pairs})
    inst_keys = sorted({key for _, key in pairs})
    m = own[base_keys[0]].shape[-1]
    n = m // 2
    carry_specs = [
        pl.BlockSpec((TILE, n), lambda i, p: (i, 0)),
        pl.BlockSpec((1, TILE), lambda i, p: (0, i)),
        pl.BlockSpec((1, n), lambda i, p: (0, 0)),
    ]
    carry_shapes = [
        jax.ShapeDtypeStruct((m, n), jnp.float32),
        jax.ShapeDtypeStruct((1, m), jnp.float32),
        jax.ShapeDtypeStruct((1, n), jnp.float32),
    ]
    depth = len(pairs) * ROWS
    call = pl.pallas_call(
        functools.partial(dot_kernel, pairs, base_keys, inst_keys, first, last, total),
        grid_spec=pltpu.PrefetchScalarGridSpec(
            num_scalar_prefetch=1,
            grid=(m // TILE,),
            in_specs=[pl.BlockSpec((8, ROWS, TILE), lambda i, p: (0, 0, i))] * len(base_keys)
            + [pl.BlockSpec(memory_space=pl.ANY)] * len(inst_keys)
            + ([] if first else carry_specs),
            out_specs=carry_specs[0] if last else carry_specs,
            scratch_shapes=[
                pltpu.VMEM((depth, n), jnp.bfloat16),
                pltpu.VMEM((1, n), jnp.float32),
                pltpu.SemaphoreType.DMA,
            ],
        ),
        out_shape=carry_shapes[0] if last else carry_shapes,
        compiler_params=pltpu.CompilerParams(vmem_limit_bytes=56 << 20),
        cost_estimate=pl.CostEstimate(
            flops=2 * depth * m * n, bytes_accessed=depth * (m + n) * 2 + 8 * m * n, transcendentals=0
        ),
        name="partial_gram",
    )

    def run(pos, base, inst, carry):
        return call(pos, *[base[k] for k in base_keys], *[inst[k] for k in inst_keys], *(carry or ()))

    keys = set(base_keys + inst_keys)
    own, mate = ({key: pieces[key] for key in keys} for pieces in (own, mate))
    return lax.cond(
        pos[4] == 0,
        lambda pos, own, mate, carry: run(pos, own, mate, carry),
        lambda pos, own, mate, carry: run(pos, mate, own, carry),
        pos,
        own,
        mate,
        carry,
    )


def send(x, target):
    return lax.ppermute(x, AXES, [(device(*p), device(*target(*p))) for p in places()])


def ring(x, way):
    return send(x, lambda z, xl, y, xh, c: (z + way * c, xl, y + way * (1 - c), xh, c))


def across(x):
    return send(x, lambda z, xl, y, xh, c: (z, xl ^ c, y, xh ^ (1 - c), c))


def mated(x):
    return send(x, lambda z, xl, y, xh, c: (z, xl, y, xh, 1 - c))


def per_device(base_pre, inst_pre, base_support, inst_support):
    total = base_pre.shape[0] * 128
    tie = lax.optimization_barrier

    def after(x, *others):
        return tie((x, others))[0]

    row, column = lax.axis_index("base"), lax.axis_index("inst")
    pos = jnp.stack([row // 2, row % 2, column // 4, column // 2 % 2, column % 2]).astype(jnp.int32)
    codes = [base_pre, inst_pre, base_support, inst_support]
    groups = [
        [device(z, xl, y, xh, 0) for z in range(4) for xl in range(2)] for y in range(4) for xh in range(2)
    ] + [[device(z, xl, y, xh, 1) for y in range(4) for xh in range(2)] for z in range(4) for xl in range(2)]

    def spread(x):
        return lax.all_to_all(x, AXES, 0, 0, axis_index_groups=groups, tiled=True)

    staying = emphasize(0, pos, *codes)
    leaving = emphasize(1, after(pos, staying), *codes)
    a = spread(staying)
    leaving, a = tie((leaving, a))
    arriving = mated(leaving)
    a3, a1 = ring(a, 1), ring(a, -1)
    xa = across(a)
    b = spread(arriving)
    a2 = ring(a3, 1)
    b3, b1 = ring(b, 1), ring(b, -1)
    b2 = ring(b1, -1)
    xa = after(xa, b3, b1, a2)
    xb = across(after(b, xa))
    xa3, xa1 = ring(xa, 1), ring(xa, -1)
    xb = after(xb, xa3, xa1, b2)
    xb3, xb1 = ring(xb, 1), ring(xb, -1)
    xa2 = ring(xa3, 1)
    own = {(0, 0, 0): a, (1, 0, 0): a1, (2, 0, 0): a2, (3, 0, 0): a3}
    own |= {(0, 0, 1): b, (1, 0, 1): b1, (2, 0, 1): b2, (3, 0, 1): b3}
    mate = {key: mated(x) for key, x in own.items()}
    steps = [(k, dx) for k in range(4) for dx in range(2)]
    blocks = [(p + (t,), q + (1 - t,)) for t in range(2) for q in steps for p in steps]
    early = [(p, q) for p, q in blocks if p[1] == 0 and q[1] == 0]
    ready = [(p, q) for p, q in blocks if {p[1:], q[1:]} in ({(0, 0), (0, 1)}, {(1, 0), (0, 1)}) and (2, 1) not in (p[:2], q[:2])]
    middle = [pair for pair in ready if pair not in early]
    late = [pair for pair in blocks if pair not in ready]
    carry = partial_gram(after(pos, xb), own, mate, early, None, False, total)
    xb3, xb1, carry = tie((xb3, xb1, carry))
    xb2 = ring(xb1, -1)
    more = {(0, 1, 0): xa, (1, 1, 0): xa1, (3, 1, 0): xa3}
    own |= more
    mate |= {key: mated(x) for key, x in more.items()}
    carry = partial_gram(pos, own, mate, middle, carry, False, total)
    xb2, carry = tie((xb2, carry))
    more = {(2, 1, 0): xa2, (0, 1, 1): xb, (1, 1, 1): xb1, (2, 1, 1): xb2, (3, 1, 1): xb3}
    own |= more
    mate |= {key: mated(x) for key, x in more.items()}
    return partial_gram(pos, own, mate, late, carry, True, total)


def solution(mesh):
    spec = P(AXES, None)
    return jax.shard_map(
        per_device, mesh=mesh, in_specs=(spec,) * 4, out_specs=P("base", "inst"), check_vma=False
    )
```

```python
import functools

import jax
import jax.numpy as jnp
from jax import lax
from jax.experimental import pallas as pl
from jax.experimental.pallas import tpu as pltpu
from jax.sharding import PartitionSpec as P

AXES = ("base", "inst")
SIZES = (4, 2, 4, 2, 2)
TILE = 512
ROWS = 32


def device(z, xl, y, xh, c):
    return (((z % 4) * 2 + xl) * 4 + y % 4) * 4 + xh * 2 + c


def places():
    return [(z, xl, y, xh, c) for z in range(4) for xl in range(2) for y in range(4) for xh in range(2) for c in range(2)]


def emphasize_kernel(side, base_ref, inst_ref, base_sup_ref, inst_sup_ref, out_ref, pre_ref, support_ref, mask_ref, sem):
    for own, pre, sup in ((side, base_ref, base_sup_ref), (1 - side, inst_ref, inst_sup_ref)):

        @pl.when(lax.axis_index("inst") % 2 == own)
        def _(pre=pre, sup=sup):
            pltpu.make_async_copy(sup, support_ref, sem.at[0]).start()
            pltpu.make_async_copy(pre, pre_ref, sem.at[1]).start()

    pltpu.make_async_copy(base_sup_ref, support_ref, sem.at[0]).wait()
    toks, latents = pre_ref.shape
    active = support_ref.shape[1]
    groups = latents // 128
    per_block = groups // 8
    rows = lax.broadcasted_iota(jnp.int32, (groups, active), 0)
    lanes = lax.broadcasted_iota(jnp.int32, (128, active), 0)

    def token(t, carry):
        picks = support_ref[pl.ds(t, 1), :]
        high = (rows == (picks >> 7)).astype(jnp.bfloat16)
        low = (lanes == (picks & 127)).astype(jnp.bfloat16)
        mask_ref[pl.ds(t * groups, groups), :] = lax.dot_general(
            high, low, (((1,), (1,)), ((), ())), preferred_element_type=jnp.float32
        )
        return carry

    lax.fori_loop(0, toks, token, 0, unroll=32)
    pltpu.make_async_copy(base_ref, pre_ref, sem.at[1]).wait()
    total = jnp.zeros((toks, 128), jnp.float32)
    for g in range(groups):
        wide = pre_ref[:, g * 128 : (g + 1) * 128].astype(jnp.float32)
        total = total + wide * wide
    scale = lax.rsqrt(jnp.sum(total, axis=1, keepdims=True) / latents + 1e-06)
    for g in range(groups):
        wide = pre_ref[:, g * 128 : (g + 1) * 128].astype(jnp.float32)
        on = mask_ref[pl.ds(g, toks, stride=groups), :]
        block, place = g // per_block, g % per_block * 128
        out_ref[block, :, place : place + 128] = (wide * scale * (1.0 + 3.0 * on)).astype(jnp.bfloat16)


def emphasize(side, base_pre, inst_pre, base_support, inst_support):
    toks, latents = base_pre.shape
    return pl.pallas_call(
        functools.partial(emphasize_kernel, side),
        out_shape=jax.ShapeDtypeStruct((8, toks, latents // 8), jnp.bfloat16),
        in_specs=[pl.BlockSpec(memory_space=pl.ANY)] * 4,
        out_specs=pl.BlockSpec(memory_space=pltpu.VMEM),
        scratch_shapes=[
            pltpu.VMEM(base_pre.shape, base_pre.dtype),
            pltpu.VMEM(base_support.shape, base_support.dtype),
            pltpu.VMEM((toks * (latents // 128), 128), jnp.float32),
            pltpu.SemaphoreType.DMA((2,)),
        ],
        compiler_params=pltpu.CompilerParams(vmem_limit_bytes=56 << 20),
        cost_estimate=pl.CostEstimate(flops=1 << 30, bytes_accessed=4 << 20, transcendentals=0),
        name="emphasize",
    )(base_pre, inst_pre, base_support, inst_support)


def dot_kernel(pairs, base_keys, inst_keys, first, last, total, *refs):
    pos, refs = refs[0], list(refs[1:])
    base = {key: refs.pop(0) for key in base_keys}
    inst = {key: refs.pop(0) for key in inst_keys}
    if not first:
        acc_ref, bsq_ref, isq_ref = refs[:3]
        del refs[:3]
    if last:
        out_ref, rhs_ref, isum_ref, sem = refs
    else:
        out_ref, bsq_out, isq_out, rhs_ref, isum_ref, sem = refs
    z, xl, y, xh, c = (pos[i] for i in range(5))
    n = rhs_ref.shape[1]

    @pl.when(pl.program_id(0) == 0)
    def _():
        columns = pl.ds(pl.multiple_of(c * n, n), n)
        copies = []
        for row, ((dy, other, _), key, u) in enumerate(pairs):
            source = inst[key].at[((y + dy) & 3) * 2 + (u ^ other ^ xl ^ xh), :, columns]
            copies.append(pltpu.make_async_copy(source, rhs_ref.at[pl.ds(row * ROWS, ROWS)], sem))
        for copy in copies:
            copy.start()
        for copy in copies:
            copy.wait()
        sums = jnp.zeros((8, n), jnp.float32)
        for row in range(len(pairs)):
            wide = rhs_ref[row * ROWS : (row + 1) * ROWS, :].astype(jnp.float32)
            sums = sums + jnp.sum((wide * wide).reshape(4, 8, -1), axis=0)
        sums = jnp.sum(sums, axis=0, keepdims=True)
        isum_ref[...] = sums if first else sums + isq_ref[...]

    blocks = []
    sums = jnp.zeros((8, TILE), jnp.float32)
    for key, (dz, _, _), u in pairs:
        rows = base[key][((z + dz) & 3) * 2 + u]
        blocks.append(rows)
        wide = rows.astype(jnp.float32)
        sums = sums + jnp.sum((wide * wide).reshape(4, 8, -1), axis=0)
    sums = jnp.sum(sums, axis=0, keepdims=True)
    if not first:
        sums = sums + bsq_ref[...]
    gram = lax.dot_general(
        jnp.concatenate(blocks, axis=0),
        rhs_ref[...],
        (((0,), (0,)), ((), ())),
        preferred_element_type=jnp.float32,
    )
    if not first:
        gram = gram + acc_ref[...]
    if last:
        base_inv = 1.0 / (jnp.sqrt(sums / total + 1e-06) * jnp.sqrt(jnp.float32(total)))
        inst_inv = 1.0 / jnp.sqrt(isum_ref[...] / total + 1e-06)
        column = jnp.transpose(jnp.broadcast_to(base_inv, (8, TILE)))[:, :1]
        out_ref[...] = gram * column * inst_inv
    else:
        out_ref[...] = gram
        bsq_out[...] = sums
        isq_out[...] = isum_ref[...]


def partial_gram(pos, own, mate, pairs, carry, last, total):
    first = carry is None
    base_keys = sorted({pair[0] for pair in pairs})
    inst_keys = sorted({pair[1] for pair in pairs})
    m = own[base_keys[0]].shape[-1]
    n = m // 2
    carry_specs = [
        pl.BlockSpec((TILE, n), lambda i, p: (i, 0)),
        pl.BlockSpec((1, TILE), lambda i, p: (0, i)),
        pl.BlockSpec((1, n), lambda i, p: (0, 0)),
    ]
    carry_shapes = [
        jax.ShapeDtypeStruct((m, n), jnp.float32),
        jax.ShapeDtypeStruct((1, m), jnp.float32),
        jax.ShapeDtypeStruct((1, n), jnp.float32),
    ]
    depth = len(pairs) * ROWS
    call = pl.pallas_call(
        functools.partial(dot_kernel, pairs, base_keys, inst_keys, first, last, total),
        grid_spec=pltpu.PrefetchScalarGridSpec(
            num_scalar_prefetch=1,
            grid=(m // TILE,),
            in_specs=[pl.BlockSpec((8, ROWS, TILE), lambda i, p: (0, 0, i))] * len(base_keys)
            + [pl.BlockSpec(memory_space=pl.ANY)] * len(inst_keys)
            + ([] if first else carry_specs),
            out_specs=carry_specs[0] if last else carry_specs,
            scratch_shapes=[
                pltpu.VMEM((depth, n), jnp.bfloat16),
                pltpu.VMEM((1, n), jnp.float32),
                pltpu.SemaphoreType.DMA,
            ],
        ),
        out_shape=carry_shapes[0] if last else carry_shapes,
        compiler_params=pltpu.CompilerParams(vmem_limit_bytes=56 << 20),
        cost_estimate=pl.CostEstimate(
            flops=2 * depth * m * n, bytes_accessed=depth * (m + n) * 2 + 8 * m * n, transcendentals=0
        ),
        name="partial_gram",
    )

    def run(pos, base, inst, carry):
        return call(pos, *[base[k] for k in base_keys], *[inst[k] for k in inst_keys], *(carry or ()))

    keys = set(base_keys + inst_keys)
    own, mate = ({key: pieces[key] for key in keys} for pieces in (own, mate))
    return lax.cond(
        pos[4] == 0,
        lambda pos, own, mate, carry: run(pos, own, mate, carry),
        lambda pos, own, mate, carry: run(pos, mate, own, carry),
        pos,
        own,
        mate,
        carry,
    )


def send(x, target):
    return lax.ppermute(x, AXES, [(device(*p), device(*target(*p))) for p in places()])


def ring(x, way):
    return send(x, lambda z, xl, y, xh, c: (z + way * c, xl, y + way * (1 - c), xh, c))


def across(x):
    return send(x, lambda z, xl, y, xh, c: (z, xl ^ c, y, xh ^ (1 - c), c))


def mated(x):
    return send(x, lambda z, xl, y, xh, c: (z, xl, y, xh, 1 - c))


def per_device(base_pre, inst_pre, base_support, inst_support):
    total = base_pre.shape[0] * 128
    tie = lax.optimization_barrier

    def after(x, *others):
        return tie((x, others))[0]

    row, column = lax.axis_index("base"), lax.axis_index("inst")
    pos = jnp.stack([row // 2, row % 2, column // 4, column // 2 % 2, column % 2]).astype(jnp.int32)
    codes = [base_pre, inst_pre, base_support, inst_support]
    groups = [
        [device(z, xl, y, xl ^ p, 0) for z in range(4) for xl in range(2)] for y in range(4) for p in range(2)
    ] + [[device(z, xh ^ p, y, xh, 1) for y in range(4) for xh in range(2)] for z in range(4) for p in range(2)]

    def spread(x):
        return lax.all_to_all(x, AXES, 0, 0, axis_index_groups=groups, tiled=True)

    staying = emphasize(0, *codes)
    leaving = emphasize(1, *after(codes, staying))
    a = spread(staying)
    leaving, a = tie((leaving, a))
    arriving = mated(leaving)
    a3, a1 = ring(a, 1), ring(a, -1)
    xa = across(a)
    b = spread(arriving)
    a2 = ring(a3, 1)
    b3, b1 = ring(b, 1), ring(b, -1)
    b2 = ring(b1, -1)
    xb = across(after(b, xa))
    xa = after(xa, a2)
    xa3, xa1 = ring(xa, 1), ring(xa, -1)
    xb = after(xb, xa3, xa1)
    xb3, xb1 = ring(xb, 1), ring(xb, -1)
    xa2 = ring(xa3, 1)
    own = {(0, 0, 0): a, (1, 0, 0): a1, (2, 0, 0): a2, (3, 0, 0): a3}
    own |= {(0, 0, 1): b, (1, 0, 1): b1, (2, 0, 1): b2, (3, 0, 1): b3}
    mate = {key: mated(x) for key, x in own.items()}
    blocks = [
        ((k, d, t), (q, d, 1 - t), u)
        for d in range(2) for t in range(2) for q in range(4) for k in range(4) for u in range(2)
    ]
    early = [pair for pair in blocks if pair[0][1] == 0]
    middle = [pair for pair in blocks if pair[0][1] == 1 and 2 not in (pair[0][0], pair[1][0])]
    late = [pair for pair in blocks if pair not in early + middle]
    carry = partial_gram(after(pos, xb), own, mate, early, None, False, total)
    xb3, xb1, carry = tie((xb3, xb1, carry))
    xb2 = ring(xb1, -1)
    more = {(0, 1, 0): xa, (1, 1, 0): xa1, (3, 1, 0): xa3}
    more |= {(0, 1, 1): xb, (1, 1, 1): xb1, (3, 1, 1): xb3}
    own |= more
    mate |= {key: mated(x) for key, x in more.items()}
    carry = partial_gram(pos, own, mate, middle, carry, False, total)
    xb2, xa2, carry = tie((xb2, xa2, carry))
    more = {(2, 1, 0): xa2, (2, 1, 1): xb2}
    own |= more
    mate |= {key: mated(x) for key, x in more.items()}
    return partial_gram(pos, own, mate, late, carry, True, total)


def solution(mesh):
    spec = P(AXES, None)
    return jax.shard_map(
        per_device, mesh=mesh, in_specs=(spec,) * 4, out_specs=P("base", "inst"), check_vma=False
    )
```

```python
import functools

import jax
import jax.numpy as jnp
from jax import lax
from jax.experimental import pallas as pl
from jax.experimental.pallas import tpu as pltpu
from jax.sharding import PartitionSpec as P

AXES = ("base", "inst")
SIZES = (4, 2, 4, 2, 2)
TILE = 512
ROWS = 32


def device(z, xl, y, xh, c):
    return (((z % 4) * 2 + xl) * 4 + y % 4) * 4 + xh * 2 + c


def places():
    return [(z, xl, y, xh, c) for z in range(4) for xl in range(2) for y in range(4) for xh in range(2) for c in range(2)]


def emphasize_kernel(side, base_ref, inst_ref, base_sup_ref, inst_sup_ref, out_ref, pre_ref, support_ref, mask_ref, sem):
    for own, pre, sup in ((side, base_ref, base_sup_ref), (1 - side, inst_ref, inst_sup_ref)):

        @pl.when(lax.axis_index("inst") % 2 == own)
        def _(pre=pre, sup=sup):
            pltpu.make_async_copy(sup, support_ref, sem.at[0]).start()
            pltpu.make_async_copy(pre, pre_ref, sem.at[1]).start()

    pltpu.make_async_copy(base_sup_ref, support_ref, sem.at[0]).wait()
    toks, latents = pre_ref.shape
    active = support_ref.shape[1]
    groups = latents // 128
    per_block = groups // 8
    rows = lax.broadcasted_iota(jnp.int32, (groups, active), 0)
    lanes = lax.broadcasted_iota(jnp.int32, (128, active), 0)

    def token(t, carry):
        picks = support_ref[pl.ds(t, 1), :]
        high = (rows == (picks >> 7)).astype(jnp.bfloat16)
        low = (lanes == (picks & 127)).astype(jnp.bfloat16)
        mask_ref[pl.ds(t * groups, groups), :] = lax.dot_general(
            high, low, (((1,), (1,)), ((), ())), preferred_element_type=jnp.float32
        )
        return carry

    lax.fori_loop(0, toks, token, 0, unroll=32)
    pltpu.make_async_copy(base_ref, pre_ref, sem.at[1]).wait()
    total = jnp.zeros((toks, 128), jnp.float32)
    for g in range(groups):
        wide = pre_ref[:, g * 128 : (g + 1) * 128].astype(jnp.float32)
        total = total + wide * wide
    scale = lax.rsqrt(jnp.sum(total, axis=1, keepdims=True) / latents + 1e-06)
    for g in range(groups):
        wide = pre_ref[:, g * 128 : (g + 1) * 128].astype(jnp.float32)
        on = mask_ref[pl.ds(g, toks, stride=groups), :]
        block, place = g // per_block, g % per_block * 128
        out_ref[block, :, place : place + 128] = (wide * scale * (1.0 + 3.0 * on)).astype(jnp.bfloat16)


def emphasize(side, base_pre, inst_pre, base_support, inst_support):
    toks, latents = base_pre.shape
    return pl.pallas_call(
        functools.partial(emphasize_kernel, side),
        out_shape=jax.ShapeDtypeStruct((8, toks, latents // 8), jnp.bfloat16),
        in_specs=[pl.BlockSpec(memory_space=pl.ANY)] * 4,
        out_specs=pl.BlockSpec(memory_space=pltpu.VMEM),
        scratch_shapes=[
            pltpu.VMEM(base_pre.shape, base_pre.dtype),
            pltpu.VMEM(base_support.shape, base_support.dtype),
            pltpu.VMEM((toks * (latents // 128), 128), jnp.float32),
            pltpu.SemaphoreType.DMA((2,)),
        ],
        compiler_params=pltpu.CompilerParams(vmem_limit_bytes=56 << 20),
        cost_estimate=pl.CostEstimate(flops=1 << 30, bytes_accessed=4 << 20, transcendentals=0),
        name="emphasize",
    )(base_pre, inst_pre, base_support, inst_support)


def dot_kernel(pairs, base_keys, inst_keys, first, last, total, *refs):
    pos, refs = refs[0], list(refs[1:])
    base = {key: refs.pop(0) for key in base_keys}
    inst = {key: refs.pop(0) for key in inst_keys}
    if not first:
        acc_ref, bsq_ref, isq_ref = refs[:3]
        del refs[:3]
    if last:
        out_ref, rhs_ref, isum_ref, sem = refs
    else:
        out_ref, bsq_out, isq_out, rhs_ref, isum_ref, sem = refs
    z, xl, y, xh, c = (pos[i] for i in range(5))
    n = rhs_ref.shape[1]

    @pl.when(pl.program_id(0) == 0)
    def _():
        columns = pl.ds(pl.multiple_of(c * n, n), n)
        copies = []
        for row, ((dy, other, _), key, u) in enumerate(pairs):
            source = inst[key].at[((y + dy) & 3) * 2 + (u ^ other ^ xl ^ xh), :, columns]
            copies.append(pltpu.make_async_copy(source, rhs_ref.at[pl.ds(row * ROWS, ROWS)], sem))
        for copy in copies:
            copy.start()
        for copy in copies:
            copy.wait()
        sums = jnp.zeros((8, n), jnp.float32)
        for row in range(len(pairs)):
            wide = rhs_ref[row * ROWS : (row + 1) * ROWS, :].astype(jnp.float32)
            sums = sums + jnp.sum((wide * wide).reshape(4, 8, -1), axis=0)
        sums = jnp.sum(sums, axis=0, keepdims=True)
        isum_ref[...] = sums if first else sums + isq_ref[...]

    blocks = []
    sums = jnp.zeros((8, TILE), jnp.float32)
    for key, (dz, _, _), u in pairs:
        rows = base[key][u if base[key].shape[0] == 2 else ((z + dz) & 3) * 2 + u]
        blocks.append(rows)
        wide = rows.astype(jnp.float32)
        sums = sums + jnp.sum((wide * wide).reshape(4, 8, -1), axis=0)
    sums = jnp.sum(sums, axis=0, keepdims=True)
    if not first:
        sums = sums + bsq_ref[...]
    gram = lax.dot_general(
        jnp.concatenate(blocks, axis=0),
        rhs_ref[...],
        (((0,), (0,)), ((), ())),
        preferred_element_type=jnp.float32,
    )
    if not first:
        gram = gram + acc_ref[...]
    if last:
        base_inv = 1.0 / (jnp.sqrt(sums / total + 1e-06) * jnp.sqrt(jnp.float32(total)))
        inst_inv = 1.0 / jnp.sqrt(isum_ref[...] / total + 1e-06)
        column = jnp.transpose(jnp.broadcast_to(base_inv, (8, TILE)))[:, :1]
        out_ref[...] = gram * column * inst_inv
    else:
        out_ref[...] = gram
        bsq_out[...] = sums
        isq_out[...] = isum_ref[...]


def partial_gram(pos, own, mate, pairs, carry, last, total):
    first = carry is None
    base_keys = sorted({pair[0] for pair in pairs})
    inst_keys = sorted({pair[1] for pair in pairs})
    m = own[base_keys[0]].shape[-1]
    n = m // 2
    carry_specs = [
        pl.BlockSpec((TILE, n), lambda i, p: (i, 0)),
        pl.BlockSpec((1, TILE), lambda i, p: (0, i)),
        pl.BlockSpec((1, n), lambda i, p: (0, 0)),
    ]
    carry_shapes = [
        jax.ShapeDtypeStruct((m, n), jnp.float32),
        jax.ShapeDtypeStruct((1, m), jnp.float32),
        jax.ShapeDtypeStruct((1, n), jnp.float32),
    ]
    base_specs = []
    for key in base_keys:
        steps = {pair[1][0] for pair in pairs if pair[0] == key}
        if len(steps) == 1:
            index = lambda i, p, dz=min(steps): ((p[0] + dz) & 3, 0, i)
            base_specs.append(pl.BlockSpec((2, ROWS, TILE), index))
        else:
            base_specs.append(pl.BlockSpec((8, ROWS, TILE), lambda i, p: (0, 0, i)))
    depth = len(pairs) * ROWS
    call = pl.pallas_call(
        functools.partial(dot_kernel, pairs, base_keys, inst_keys, first, last, total),
        grid_spec=pltpu.PrefetchScalarGridSpec(
            num_scalar_prefetch=1,
            grid=(m // TILE,),
            in_specs=base_specs
            + [pl.BlockSpec(memory_space=pl.ANY)] * len(inst_keys)
            + ([] if first else carry_specs),
            out_specs=carry_specs[0] if last else carry_specs,
            scratch_shapes=[
                pltpu.VMEM((depth, n), jnp.bfloat16),
                pltpu.VMEM((1, n), jnp.float32),
                pltpu.SemaphoreType.DMA,
            ],
        ),
        out_shape=carry_shapes[0] if last else carry_shapes,
        compiler_params=pltpu.CompilerParams(vmem_limit_bytes=56 << 20),
        cost_estimate=pl.CostEstimate(
            flops=2 * depth * m * n, bytes_accessed=depth * (m + n) * 2 + 8 * m * n, transcendentals=0
        ),
        name="partial_gram",
    )

    def run(pos, base, inst, carry):
        return call(pos, *[base[k] for k in base_keys], *[inst[k] for k in inst_keys], *(carry or ()))

    keys = set(base_keys + inst_keys)
    own, mate = ({key: pieces[key] for key in keys} for pieces in (own, mate))
    return lax.cond(
        pos[4] == 0,
        lambda pos, own, mate, carry: run(pos, own, mate, carry),
        lambda pos, own, mate, carry: run(pos, mate, own, carry),
        pos,
        own,
        mate,
        carry,
    )


def send(x, target):
    return lax.ppermute(x, AXES, [(device(*p), device(*target(*p))) for p in places()])


def ring(x, way):
    return send(x, lambda z, xl, y, xh, c: (z + way * c, xl, y + way * (1 - c), xh, c))


def across(x):
    return send(x, lambda z, xl, y, xh, c: (z, xl ^ c, y, xh ^ (1 - c), c))


def mated(x):
    return send(x, lambda z, xl, y, xh, c: (z, xl, y, xh, 1 - c))


def per_device(base_pre, inst_pre, base_support, inst_support):
    total = base_pre.shape[0] * 128
    tie = lax.optimization_barrier

    def after(x, *others):
        return tie((x, others))[0]

    row, column = lax.axis_index("base"), lax.axis_index("inst")
    pos = jnp.stack([row // 2, row % 2, column // 4, column // 2 % 2, column % 2]).astype(jnp.int32)
    codes = [base_pre, inst_pre, base_support, inst_support]
    groups = [
        [device(z, xl, y, xl ^ p, 0) for z in range(4) for xl in range(2)] for y in range(4) for p in range(2)
    ] + [[device(z, xh ^ p, y, xh, 1) for y in range(4) for xh in range(2)] for z in range(4) for p in range(2)]

    def spread(x):
        return lax.all_to_all(x, AXES, 0, 0, axis_index_groups=groups, tiled=True)

    staying = emphasize(0, *codes)
    leaving = emphasize(1, *after(codes, staying))
    a = spread(staying)
    leaving, a = tie((leaving, a))
    arriving = mated(leaving)
    a3, a1 = ring(a, 1), ring(a, -1)
    xa = across(a)
    b = spread(arriving)
    a2 = ring(a3, 1)
    b3, b1 = ring(b, 1), ring(b, -1)
    b2 = ring(b1, -1)
    xb = across(after(b, xa))
    xa = after(xa, a2)
    xa3, xa1 = ring(xa, 1), ring(xa, -1)
    xb = after(xb, xa3, xa1)
    xb3, xb1 = ring(xb, 1), ring(xb, -1)
    xa2 = ring(xa3, 1)
    own = {(0, 0, 0): a, (1, 0, 0): a1, (2, 0, 0): a2, (3, 0, 0): a3}
    own |= {(0, 0, 1): b, (1, 0, 1): b1, (2, 0, 1): b2, (3, 0, 1): b3}
    mate = {key: mated(x) for key, x in own.items()}
    blocks = [
        ((k, d, t), (q, d, 1 - t), u)
        for d in range(2) for t in range(2) for q in range(4) for k in range(4) for u in range(2)
    ]
    early = [pair for pair in blocks if pair[0][1] == 0]
    middle = [pair for pair in blocks if pair[0][1] == 1 and 2 not in (pair[0][0], pair[1][0])]
    late = [pair for pair in blocks if pair not in early + middle]
    carry = partial_gram(after(pos, xb), own, mate, early, None, False, total)
    xb3, xb1, carry = tie((xb3, xb1, carry))
    xb2 = ring(xb1, -1)
    more = {(0, 1, 0): xa, (1, 1, 0): xa1, (3, 1, 0): xa3}
    more |= {(0, 1, 1): xb, (1, 1, 1): xb1, (3, 1, 1): xb3}
    own |= more
    mate |= {key: mated(x) for key, x in more.items()}
    carry = partial_gram(pos, own, mate, middle, carry, False, total)
    xb2, xa2, carry = tie((xb2, xa2, carry))
    more = {(2, 1, 0): xa2, (2, 1, 1): xb2}
    own |= more
    mate |= {key: mated(x) for key, x in more.items()}
    return partial_gram(pos, own, mate, late, carry, True, total)


def solution(mesh):
    spec = P(AXES, None)
    return jax.shard_map(
        per_device, mesh=mesh, in_specs=(spec,) * 4, out_specs=P("base", "inst"), check_vma=False
    )
```
